256 devices in a mesh: dp: 16 (over z, core), ulysses: 8 (over y, x_hi), tensor: 2 (over x_lo).
Axes of the slice: x: 4 (x_hi: 2, x_lo: 2; x = x_hi * 2 + x_lo), y: 4, z: 8, core: 2. Of those that a mesh axis runs over, the one named last changes fastest.
Arguments:
- queries: bfloat16 [49152, 2048], P(('dp', 'ulysses'), 'tensor'), parts along dimension 0, may hold values from -128 to 128
- key_vectors: bfloat16 [49152, 2048], P(('dp', 'ulysses'), 'tensor'), parts along dimension 0, may hold values from -6 to 6
- value_vectors: bfloat16 [49152, 2048], P(('dp', 'ulysses'), 'tensor'), parts along dimension 0, may hold values from -6 to 6
- window_tiles: int32 [128, 6], P('dp'), parts along dimension 0, may hold values from -1 to 7, as said below
- out_weight: bfloat16 [2048, 3072], P('tensor', 'ulysses'), may hold values from -0.1875 to 0.1875
Outputs:
- mixed: bfloat16 [49152, 3072], P(('dp', 'ulysses'), 'tensor'), parts along dimension 0
The draws below stay inside these ranges and needn't reach their ends.
There are 16 independent parts, one for each index of `dp`. The reference program is written for one: setup_inputs(seed, part) draws one part's arguments, and reference() takes and returns one part's arrays. A program takes and returns all parts, laid end to end along the dimension named above; an argument that names none is the same for every part. Nothing has to cross between parts.
Inputs may be any that keep to these rules, and one draw needn't show every extreme that they name: `window_tiles`: tiles form a grid of 4 x 1 x 2 (time slowest; tile t*2 + h*2 + w). Row i lists, in an order drawn from the seed, tile i itself and a subset drawn from the seed of the tiles whose three grid positions each differ from tile i's by at most one, each listed at most once; the remaining slots hold -1.
All inputs are finite; a program needn't handle non-finite values.
Results may differ from the reference program's by a relative error of at most 0.0057.
Values may be sent and summed in bfloat16 or wider, within the bound.
A program may use at most 64 MiB of HBM per device.

```python
import jax
import jax.numpy as jnp
from jax import lax

D = 3072
HEADS = 16
HD = 128
TILE = 384
GH = 1
GW = 2
TILES = 8
GT = 4
WMAX = 6
TOKENS = 3072


def shared_rows(key):
    first, second = jax.random.split(key, 2)
    query_base = jax.random.truncated_normal(first, -4.5, 4.5, (TOKENS, HEADS * HD), jnp.float32)
    key_base = jax.random.truncated_normal(second, -4.5, 4.5, (TOKENS, HEADS * HD), jnp.float32)
    return (query_base, key_base)


def draw_queries(key, part):
    query_base, key_base = shared_rows(key)
    values = query_base
    return values.astype(jnp.bfloat16)


def draw_key_vectors(key, part):
    query_base, key_base = shared_rows(key)
    values = key_base
    return values.astype(jnp.bfloat16)


def draw_window_tiles(key, part):
    key = jax.random.fold_in(key, 17)
    keep_key, order_key = jax.random.split(key)
    tile_index = jnp.arange(TILES)
    time_pos = tile_index // (GH * GW)
    row_pos = tile_index // GW % GH
    col_pos = tile_index % GW
    candidates = []
    allowed = []
    for step_t in (-1, 0, 1):
        for step_h in (-1, 0, 1):
            for step_w in (-1, 0, 1):
                new_t = time_pos + step_t
                new_h = row_pos + step_h
                new_w = col_pos + step_w
                inside = (new_t >= 0) & (new_t < GT) & (new_h >= 0) & (new_h < GH) & (new_w >= 0) & (new_w < GW)
                candidates.append(new_t * GH * GW + new_h * GW + new_w)
                allowed.append(inside)
    candidates = jnp.stack(candidates, axis=1)
    allowed = jnp.stack(allowed, axis=1)
    itself = candidates == tile_index[:, None]
    keep_roll = jax.random.randint(keep_key, (TILES, 27), 0, 4)
    allowed = allowed & ((keep_roll >= 1) | itself)
    order = jnp.argsort(jnp.where(allowed, 0, 1), axis=1, stable=True)[:, :WMAX]
    picked = jnp.take_along_axis(candidates, order, axis=1)
    kept = jnp.take_along_axis(allowed, order, axis=1)
    picked = jnp.where(kept, picked, -1)
    row_keys = jax.random.split(order_key, TILES)
    shuffle = jax.vmap(lambda row_key: jax.random.permutation(row_key, WMAX))(row_keys)
    return jnp.take_along_axis(picked, shuffle, axis=1).astype(jnp.int32)


def spiked(values, own_key, source, target, shards_of, factor):
    def block_of(axis_at):
        return (jnp.arange(values.shape[axis_at]) // (values.shape[axis_at] // shards_of)).reshape((-1,) + (1,) * (values.ndim - 1 - axis_at))

    first = jax.random.permutation(own_key, shards_of)[block_of(target)]
    second = (block_of(target) + shards_of // 2) % shards_of
    return jnp.where((block_of(source) == first) | (block_of(source) == second), factor * values, values)


def shard_levels(own_key, extent, cuts, low, largest):
    loudness = 1.0
    for position, parts in cuts:
        draws = jax.random.uniform(jax.random.fold_in(jax.random.fold_in(own_key, 6), position), (parts,), jnp.float32, low / len(cuts), largest / len(cuts))
        loudness = loudness * jnp.repeat(jnp.exp(draws), extent[position] // parts).reshape((-1,) + (1,) * (len(extent) - 1 - position))
    return loudness


def bell_draw(key, extent, scale, bound, cuts=(), dtype=jnp.bfloat16):
    factor_of = shard_levels(key, extent, cuts, -0.22, 0.18) if cuts else 1.0
    drawn = jax.random.normal(key, extent, jnp.float32) * scale * factor_of
    return jnp.minimum(jnp.maximum(drawn, -bound), bound).astype(dtype)


def gaussian_with(own_key, extent, scale, most, shards, heavy, held_as=jnp.bfloat16):
    entries = scale * jax.random.normal(own_key, extent, jnp.float32)
    if shards:
        entries = entries * shard_levels(own_key, extent, shards, -0.22, 0.18)
    return jnp.clip(spiked(entries, jax.random.fold_in(own_key, 3), *heavy), -most, most).astype(held_as)


def setup_inputs(seed: int = 0, part: int = 0) -> dict:
    streams_of = jax.random.split(jax.random.key(seed), 6)
    own_keys = jax.random.split(jax.random.fold_in(streams_of[5], part), 6)
    return {
        "queries": draw_queries(jax.random.fold_in(jax.random.fold_in(streams_of[5], part), 71), part),
        "key_vectors": draw_key_vectors(jax.random.fold_in(jax.random.fold_in(streams_of[5], part), 71), part),
        "value_vectors": bell_draw(own_keys[2], (TOKENS, HEADS * HD), 1.0, 6.0, ((0, 8), (1, 2))),
        "window_tiles": draw_window_tiles(jax.random.fold_in(jax.random.fold_in(streams_of[5], part), 71), part),
        "out_weight": gaussian_with(streams_of[4], (HEADS * HD, D), (HEADS * HD) ** -0.5, 0.1875, ((0, 2), (1, 8)), (0, 1, 8, 2.0)),
    }


def head_attention(query_head, key_head, value_head, window_tiles):
    tile_count = query_head.shape[0] // TILE
    query_tiles = query_head.reshape(tile_count, TILE, HD)
    key_tiles = key_head.reshape(tile_count, TILE, HD)
    value_tiles = value_head.reshape(tile_count, TILE, HD)
    scale = HD ** -0.5

    def per_tile(pair):
        query_tile, window = pair
        valid_slot = window >= 0
        safe_index = jnp.maximum(window, 0).astype(jnp.int32)
        key_block = key_tiles[safe_index].reshape(WMAX * TILE, HD)
        value_block = value_tiles[safe_index].reshape(WMAX * TILE, HD)
        scores = jnp.dot(query_tile, key_block.T, preferred_element_type=jnp.float32) * scale
        allowed = jnp.repeat(valid_slot, TILE)[None, :]
        scores = jnp.where(allowed, scores, -1e30)
        peak_score = jnp.max(scores, axis=1, keepdims=True)
        exp_scores = jnp.exp(scores - peak_score)
        weights = (exp_scores / jnp.sum(exp_scores, axis=1, keepdims=True)).astype(jnp.bfloat16)
        return jnp.dot(weights, value_block, preferred_element_type=jnp.float32).astype(jnp.bfloat16)

    result = lax.map(per_tile, (query_tiles, window_tiles))
    return result.reshape(tile_count * TILE, HD)


def reference(queries, key_vectors, value_vectors, window_tiles, out_weight):
    def by_head(values):
        return jnp.transpose(values.reshape(TOKENS, HEADS, HD), (1, 0, 2))

    def one_head(triple):
        return head_attention(triple[0], triple[1], triple[2], window_tiles)

    attention = lax.map(one_head, (by_head(queries), by_head(key_vectors), by_head(value_vectors)))
    attention = jnp.transpose(attention, (1, 0, 2)).reshape(TOKENS, HEADS * HD)
    return jnp.dot(attention, out_weight, preferred_element_type=jnp.float32).astype(jnp.bfloat16)
```

```python
import functools
import math

import jax
import jax.numpy as jnp
from jax import lax
from jax.experimental import pallas as pl
from jax.experimental.pallas import tpu as pltpu
from jax.sharding import PartitionSpec as P

HD = 128
TILE = 384
WMAX = 6
ROWS = 128
MESH = pl.DeviceIdType.MESH
COEF = HD ** (-0.5) * math.log2(math.e)
FAR = 1e30


def attend(tile, count, window, q_tile, k_tiles, v_tiles, scores, put):
    first = 2 * jnp.maximum(lax.div(tile, 2) - 1, 0)
    away = []
    for j in range(count):
        listed = window[tile, 0] == first + j
        for s in range(1, WMAX):
            listed = listed | (window[tile, s] == first + j)
        away.append(jnp.where(listed, 0.0, FAR).astype(jnp.float32))
    for block in range(TILE // ROWS):
        rows = pl.ds(block * ROWS, ROWS)
        held = scores.at[block % 2]
        q = q_tile[tile, rows, :]
        peak = None
        for j in range(count):
            s = lax.dot_general(
                q, k_tiles[first + j], (((1,), (1,)), ((), ())), preferred_element_type=jnp.float32
            )
            held[:, pl.ds(j * TILE, TILE)] = s
            top = jnp.maximum(jnp.maximum(s[:, :HD], s[:, HD : 2 * HD]), s[:, 2 * HD :]) - away[j]
            peak = top if peak is None else jnp.maximum(peak, top)
        peak = jnp.max(peak, axis=1, keepdims=True) * COEF
        total = None
        mixed = None
        for j in range(count):
            e = jnp.exp2(held[:, pl.ds(j * TILE, TILE)] * COEF - (peak + away[j]))
            part = e[:, :HD] + e[:, HD : 2 * HD] + e[:, 2 * HD :]
            total = part if total is None else total + part
            term = jnp.dot(
                e.astype(jnp.bfloat16), v_tiles[first + j], preferred_element_type=jnp.float32
            )
            mixed = term if mixed is None else mixed + term
        total = jnp.sum(total, axis=1, keepdims=True)
        put(rows, (mixed / total).astype(jnp.bfloat16))


def kernel(
    window, q_ref, k_ref, v_ref, w_ref, out_ref,
    qb, kb, vb, ob, done, wb, scores, acc,
    s_qkv, r_qkv, s_w, r_w, s_ring, r_ring, s_sib, r_sib, s_o, r_o,
):
    dp, u, t = lax.axis_index("dp"), lax.axis_index("ulysses"), lax.axis_index("tensor")
    z, c = lax.div(dp, 2), lax.rem(dp, 2)
    y, w = lax.div(u, 2), lax.rem(u, 2)

    def ahead(k):
        return lax.rem(y + lax.div(k, 2), 4) * 2 + lax.rem(w + lax.rem(k, 2), 2)

    def behind(k):
        return lax.rem(y + 4 - lax.div(k, 2), 4) * 2 + lax.rem(w + lax.rem(k, 2), 2)

    up = (lax.rem(z + 1, 8) * 2 + c, u, t)
    down = (lax.rem(z + 7, 8) * 2 + c, u, t)
    sibling = (z * 2 + 1 - c, u, t)

    barrier = pltpu.get_barrier_semaphore()
    for k in range(8):
        for other in range(2):
            if k or other:
                pl.semaphore_signal(
                    barrier, inc=1, device_id=(dp, ahead(k), lax.rem(t + other, 2)), device_id_type=MESH
                )
    for device in (up, down, sibling):
        pl.semaphore_signal(barrier, inc=1, device_id=device, device_id_type=MESH)
    pl.semaphore_wait(barrier, 18)

    def remote(src, dst, send, recv, device):
        return pltpu.make_async_remote_copy(
            src_ref=src, dst_ref=dst, send_sem=send, recv_sem=recv, device_id=device, device_id_type=MESH
        )

    def landed(ref, sem):
        pltpu.make_async_copy(ref, ref, sem).wait()

    side, place = lax.div(u, 4), lax.rem(u, 4)
    piece = w_ref.at[pl.ds(pl.multiple_of(z * 128 + c * 64, 64), 64), :]
    spot = wb.at[z, t, c, :, pl.ds(pl.multiple_of(place * 384, 384), 384)]
    own = side == t

    @pl.when(own)
    def _():
        pltpu.make_async_copy(piece, spot, r_w.at[t, place]).start()

    @pl.when(jnp.logical_not(own))
    def _():
        remote(piece, spot, s_w.at[0], r_w.at[t, place], (dp, u, side)).start()

    for k in range(1, 8):
        remote(piece, spot, s_w.at[k], r_w.at[t, place], (dp, ahead(k), side)).start()

    arrays = ((k_ref, kb), (v_ref, vb), (q_ref, qb))

    def cut(ref, i):
        return ref.at[:, pl.ds(pl.multiple_of(i * HD, HD), HD)]

    for a, (ref, buf) in enumerate(arrays):
        pltpu.make_async_copy(cut(ref, u), buf.at[u], r_qkv.at[a, u]).start()
        for k in range(1, 8):
            remote(
                cut(ref, ahead(k)), buf.at[u], s_qkv.at[a, k], r_qkv.at[a, u], (dp, ahead(k), t)
            ).start()

    def share(plane, half, slot):
        ref = wb.at[plane, half, c]
        remote(ref, ref, s_sib.at[slot, half], r_sib.at[plane, half], sibling).start()

    def pass_on(plane, half, way, distance):
        ref = wb.at[plane, half, c]
        remote(
            ref, ref, s_ring.at[way, distance - 1, half], r_ring.at[way, distance - 1, half],
            down if way else up,
        ).start()

    for half in range(2):
        for i in range(4):
            landed(wb.at[z, half, c, :, pl.ds(i * 384, 384)], r_w.at[half, i])
    for half in range(2):
        pass_on(z, half, 0, 1)
        pass_on(z, half, 1, 1)
    for half in range(2):
        share(z, half, 0)

    def ring(distance):
        for half in range(2):
            for way in range(2):
                if distance == 4 and half != way:
                    continue
                plane = lax.rem(z + (distance if way else 8 - distance), 8)
                landed(wb.at[plane, half, c], r_ring.at[way, distance - 1, half])
                if distance < 3 or (distance == 3 and half == way):
                    pass_on(plane, half, way, distance + 1)
                slot = 4 if distance == 4 else distance + 4 * way
                share(plane, half, slot)

    ring(1)
    for a in range(2):
        for i in range(8):
            landed(arrays[a][1].at[i], r_qkv.at[a, i])

    def step(k, carry):
        tile = ahead(k)
        landed(qb.at[tile], r_qkv.at[2, tile])

        def put(rows, value):
            done[k, rows, :] = value

        edge = (tile < 2) | (tile >= 6)

        @pl.when(edge)
        def _():
            attend(tile, 4, window, qb, kb, vb, scores, put)

        @pl.when(jnp.logical_not(edge))
        def _():
            attend(tile, 6, window, qb, kb, vb, scores, put)

        @pl.when(k == 0)
        def _():
            pltpu.make_async_copy(done.at[k], ob.at[u, t], r_o.at[u, t]).start()

        @pl.when(k > 0)
        def _():
            remote(done.at[k], ob.at[u, t], s_o.at[k, 0], r_o.at[u, t], (dp, tile, t)).start()

        remote(done.at[k], ob.at[u, t], s_o.at[k, 1], r_o.at[u, t], (dp, tile, 1 - t)).start()
        for distance, at in ((2, 0), (3, 3), (4, 6)):

            @pl.when(k == at)
            def _():
                ring(distance)

        return carry

    lax.fori_loop(0, 8, step, 0)

    for plane in range(8):
        for half in range(2):
            landed(wb.at[plane, half, 1 - c], r_sib.at[plane, half])

    def project(k, carry):
        source = behind(k)
        for half in range(2):
            landed(ob.at[source, half], r_o.at[source, half])
        rows = jnp.concatenate([ob[source, 0], ob[source, 1]], axis=1)
        for n in range(3):
            columns = pl.ds(n * 512, 512)
            term = jnp.dot(
                rows, wb[source, :, :, :, columns].reshape(256, 512), preferred_element_type=jnp.float32
            )

            @pl.when(k == 0)
            def _():
                acc[:, columns] = term

            @pl.when((k > 0) & (k < 7))
            def _():
                acc[:, columns] += term

            @pl.when(k == 7)
            def _():
                out_ref[:, columns] = (acc[:, columns] + term).astype(jnp.bfloat16)

        return carry

    lax.fori_loop(0, 8, project, 0)

    @pl.when(jnp.logical_not(own))
    def _():
        remote(piece, spot, s_w.at[0], r_w.at[t, place], (dp, u, side)).wait_send()

    for k in range(1, 8):
        remote(piece, spot, s_w.at[k], r_w.at[t, place], (dp, ahead(k), side)).wait_send()
    for a, (ref, buf) in enumerate(arrays):
        for k in range(1, 8):
            remote(
                cut(ref, ahead(k)), buf.at[u], s_qkv.at[a, k], r_qkv.at[a, u], (dp, ahead(k), t)
            ).wait_send()
    for half in range(2):
        for way in range(2):
            for distance in range(1, 5):
                if distance < 4 or half == way:
                    ref = wb.at[z, half, c]
                    remote(
                        ref, ref, s_ring.at[way, distance - 1, half], r_ring.at[way, distance - 1, half],
                        down if way else up,
                    ).wait_send()
        for slot in range(8):
            ref = wb.at[z, half, c]
            remote(ref, ref, s_sib.at[slot, half], r_sib.at[z, half], sibling).wait_send()
    for k in range(8):
        if k:
            remote(done.at[k], ob.at[u, t], s_o.at[k, 0], r_o.at[u, t], (dp, ahead(k), t)).wait_send()
        remote(done.at[k], ob.at[u, t], s_o.at[k, 1], r_o.at[u, t], (dp, ahead(k), 1 - t)).wait_send()


def on_device(queries, key_vectors, value_vectors, window_tiles, out_weight):
    dma = pltpu.SemaphoreType.DMA
    bf16, f32 = jnp.bfloat16, jnp.float32
    return pl.pallas_call(
        kernel,
        out_shape=jax.ShapeDtypeStruct((TILE, 1536), bf16),
        in_specs=[pl.BlockSpec(memory_space=pltpu.SMEM)] + [pl.BlockSpec(memory_space=pl.ANY)] * 4,
        out_specs=pl.BlockSpec(memory_space=pltpu.VMEM),
        scratch_shapes=[
            pltpu.VMEM((8, TILE, HD), bf16),
            pltpu.VMEM((8, TILE, HD), bf16),
            pltpu.VMEM((8, TILE, HD), bf16),
            pltpu.VMEM((8, 2, TILE, HD), bf16),
            pltpu.VMEM((8, TILE, HD), bf16),
            pltpu.VMEM((8, 2, 2, 64, 1536), bf16),
            pltpu.VMEM((2, ROWS, WMAX * TILE), f32),
            pltpu.VMEM((TILE, 1536), f32),
            dma((3, 8)), dma((3, 8)), dma((8,)), dma((2, 4)),
            dma((2, 4, 2)), dma((2, 4, 2)), dma((8, 2)), dma((8, 2)), dma((8, 2)), dma((8, 2)),
        ],
        compiler_params=pltpu.CompilerParams(
            collective_id=0, has_side_effects=True, vmem_limit_bytes=44 << 20
        ),
        name="tile_attention",
    )(window_tiles, queries, key_vectors, value_vectors, out_weight)


def solution(mesh):
    in_specs = (
        P(("dp", "ulysses"), "tensor"),
        P(("dp", "ulysses"), "tensor"),
        P(("dp", "ulysses"), "tensor"),
        P("dp", None),
        P("tensor", "ulysses"),
    )
    out_specs = P(("dp", "ulysses"), "tensor")
    return jax.shard_map(
        on_device, mesh=mesh, in_specs=in_specs, out_specs=out_specs, check_vma=False
    )
```

```python
import functools
import math

import jax
import jax.numpy as jnp
from jax import lax
from jax.experimental import pallas as pl
from jax.experimental.pallas import tpu as pltpu
from jax.sharding import PartitionSpec as P

HD = 128
TILE = 384
WMAX = 6
MESH = pl.DeviceIdType.MESH
COEF = HD ** (-0.5) * math.log2(math.e)
FAR = 1e30


def attend(tile, count, window, q_tile, k_tiles, v_tiles, scores, put):
    first = 2 * jnp.maximum(lax.div(tile, 2) - 1, 0)
    away = []
    for j in range(count):
        listed = window[tile, 0] == first + j
        for s in range(1, WMAX):
            listed = listed | (window[tile, s] == first + j)
        away.append(jnp.where(listed, 0.0, FAR).astype(jnp.float32))
    q = q_tile[tile]
    peak = None
    for j in range(count):
        s = lax.dot_general(
            q, k_tiles[first + j], (((1,), (1,)), ((), ())), preferred_element_type=jnp.float32
        )
        scores[:, pl.ds(j * TILE, TILE)] = s
        top = jnp.maximum(jnp.maximum(s[:, :HD], s[:, HD : 2 * HD]), s[:, 2 * HD :]) - away[j]
        peak = top if peak is None else jnp.maximum(peak, top)
    peak = jnp.max(peak, axis=1, keepdims=True) * COEF
    total = None
    mixed = None
    for j in range(count):
        e = jnp.exp2(scores[:, pl.ds(j * TILE, TILE)] * COEF - (peak + away[j]))
        part = e[:, :HD] + e[:, HD : 2 * HD] + e[:, 2 * HD :]
        total = part if total is None else total + part
        term = jnp.dot(
            e.astype(jnp.bfloat16), v_tiles[first + j], preferred_element_type=jnp.float32
        )
        mixed = term if mixed is None else mixed + term
    total = jnp.sum(total, axis=1, keepdims=True)
    put((mixed / total).astype(jnp.bfloat16))


def kernel(
    window, q_ref, k_ref, v_ref, w_ref, out_ref,
    qb, kb, vb, ob, done, wb, scores, acc,
    s_qkv, r_qkv, s_w, r_w, s_ring, r_ring, s_sib, r_sib, s_o, r_o, level, ready,
):
    dp, u, t = lax.axis_index("dp"), lax.axis_index("ulysses"), lax.axis_index("tensor")
    z, c = lax.div(dp, 2), lax.rem(dp, 2)
    y, w = lax.div(u, 2), lax.rem(u, 2)

    def ahead(k):
        return lax.rem(y + lax.div(k, 2), 4) * 2 + lax.rem(w + lax.rem(k, 2), 2)

    def behind(k):
        return lax.rem(y + 4 - lax.div(k, 2), 4) * 2 + lax.rem(w + lax.rem(k, 2), 2)

    up = (lax.rem(z + 1, 8) * 2 + c, u, t)
    down = (lax.rem(z + 7, 8) * 2 + c, u, t)
    sibling = (z * 2 + 1 - c, u, t)

    barrier = pltpu.get_barrier_semaphore()
    odd = lax.rem(z, 2)

    def tell(sem, device):
        pl.semaphore_signal(sem, inc=1, device_id=device, device_id_type=MESH)

    for k in range(8):
        for other in range(2):
            if k or other:
                tell(barrier, (dp, ahead(k), lax.rem(t + other, 2)))
    tell(barrier, sibling)

    @pl.when(odd == 0)
    def _():
        tell(barrier, up)
        tell(barrier, down)

    pl.semaphore_wait(barrier, 16 + 2 * odd)

    @pl.when(odd == 1)
    def _():
        tell(ready, up)
        tell(ready, down)

    def remote(src, dst, send, recv, device):
        return pltpu.make_async_remote_copy(
            src_ref=src, dst_ref=dst, send_sem=send, recv_sem=recv, device_id=device, device_id_type=MESH
        )

    def landed(ref, sem):
        pltpu.make_async_copy(ref, ref, sem).wait()

    side, place = lax.div(u, 4), lax.rem(u, 4)
    piece = w_ref.at[pl.ds(pl.multiple_of(z * 128 + c * 64, 64), 64), :]
    spot = wb.at[z, t, c, :, pl.ds(pl.multiple_of(place * 384, 384), 384)]
    own = side == t

    @pl.when(own)
    def _():
        pltpu.make_async_copy(piece, spot, r_w.at[t, place]).start()

    @pl.when(jnp.logical_not(own))
    def _():
        remote(piece, spot, s_w.at[0], r_w.at[t, place], (dp, u, side)).start()

    for k in range(1, 8):
        remote(piece, spot, s_w.at[k], r_w.at[t, place], (dp, ahead(k), side)).start()

    for k in range(1, 8):
        remote(piece, spot, s_w.at[k], r_w.at[t, place], (dp, ahead(k), side)).wait_send()

    @pl.when(jnp.logical_not(own))
    def _():
        remote(piece, spot, s_w.at[0], r_w.at[t, place], (dp, u, side)).wait_send()

    x = 2 * w + t
    for step in (1, 3):
        beside = lax.rem(x + step, 4)
        tell(level, (dp, 2 * y + lax.div(beside, 2), lax.rem(beside, 2)))
        tell(level, (dp, 2 * lax.rem(y + step, 4) + w, t))
    pl.semaphore_wait(level, 4)

    arrays = ((k_ref, kb), (v_ref, vb), (q_ref, qb))

    def cut(ref, i):
        return ref.at[:, pl.ds(pl.multiple_of(i * HD, HD), HD)]

    def send(a):
        ref, buf = arrays[a]
        pltpu.make_async_copy(cut(ref, u), buf.at[u], r_qkv.at[a, u]).start()
        for k in range(1, 8):
            remote(
                cut(ref, behind(k)), buf.at[u], s_qkv.at[a, k], r_qkv.at[a, u], (dp, behind(k), t)
            ).start()

    def have(a):
        for i in range(8):
            landed(arrays[a][1].at[i], r_qkv.at[a, i])

    for a in range(3):
        send(a)

    def share(plane, half, slot):
        ref = wb.at[plane, half, c]
        remote(ref, ref, s_sib.at[slot, half], r_sib.at[plane, half], sibling).start()

    def pass_on(plane, half, way, distance):
        ref = wb.at[plane, half, c]
        remote(
            ref, ref, s_ring.at[way, distance - 1, half], r_ring.at[way, distance - 1, half],
            down if way else up,
        ).start()

    for half in range(2):
        for i in range(4):
            landed(wb.at[z, half, c, :, pl.ds(i * 384, 384)], r_w.at[half, i])

    @pl.when(odd == 0)
    def _():
        pl.semaphore_wait(ready, 2)

    for half in range(2):
        pass_on(z, half, 0, 1)
        pass_on(z, half, 1, 1)
    for half in range(2):
        share(z, half, 0)

    def ring(distance):
        for half in range(2):
            for way in range(2):
                if distance == 4 and half != way:
                    continue
                plane = lax.rem(z + (distance if way else 8 - distance), 8)
                landed(wb.at[plane, half, c], r_ring.at[way, distance - 1, half])
                if distance < 3 or (distance == 3 and half == way):
                    pass_on(plane, half, way, distance + 1)
                slot = 4 if distance == 4 else distance + 4 * way
                share(plane, half, slot)

    ring(1)
    have(0)
    have(1)
    ring(2)

    def step(k, carry):
        tile = ahead(k)
        landed(qb.at[tile], r_qkv.at[2, tile])

        def put(value):
            done[k] = value

        edge = (tile < 2) | (tile >= 6)

        @pl.when(edge)
        def _():
            attend(tile, 4, window, qb, kb, vb, scores, put)

        @pl.when(jnp.logical_not(edge))
        def _():
            attend(tile, 6, window, qb, kb, vb, scores, put)

        @pl.when(k == 0)
        def _():
            pltpu.make_async_copy(done.at[k], ob.at[u, t], r_o.at[u, t]).start()

        @pl.when(k > 0)
        def _():
            remote(done.at[k], ob.at[u, t], s_o.at[k, 0], r_o.at[u, t], (dp, tile, t)).start()

        remote(done.at[k], ob.at[u, t], s_o.at[k, 1], r_o.at[u, t], (dp, tile, 1 - t)).start()
        for distance, at in ((3, 3),):

            @pl.when(k == at)
            def _():
                ring(distance)

        return carry

    lax.fori_loop(0, 8, step, 0)

    ring(4)
    for plane in range(8):
        for half in range(2):
            landed(wb.at[plane, half, 1 - c], r_sib.at[plane, half])

    def product(k, columns):
        first, second = behind(k), behind(k + 1)
        rows = jnp.concatenate([ob[first, 0], ob[first, 1], ob[second, 0], ob[second, 1]], axis=1)
        part = [wb[source, :, :, :, columns].reshape(256, 512) for source in (first, second)]
        return jnp.dot(rows, jnp.concatenate(part, axis=0), preferred_element_type=jnp.float32)

    def arrived(k):
        for i in range(2):
            for half in range(2):
                landed(ob.at[behind(k + i), half], r_o.at[behind(k + i), half])

    def project(g, carry):
        arrived(2 * g)
        for n in range(3):
            columns = pl.ds(n * 512, 512)
            acc[:, columns] += product(2 * g, columns)
        return carry

    acc[...] = jnp.zeros_like(acc)
    lax.fori_loop(0, 3, project, 0)
    arrived(6)
    for n in range(3):
        columns = pl.ds(n * 512, 512)
        out_ref[:, columns] = (acc[:, columns] + product(6, columns)).astype(jnp.bfloat16)

    for a, (ref, buf) in enumerate(arrays):
        for k in range(1, 8):
            remote(
                cut(ref, behind(k)), buf.at[u], s_qkv.at[a, k], r_qkv.at[a, u], (dp, behind(k), t)
            ).wait_send()
    for half in range(2):
        for way in range(2):
            for distance in range(1, 5):
                if distance < 4 or half == way:
                    ref = wb.at[z, half, c]
                    remote(
                        ref, ref, s_ring.at[way, distance - 1, half], r_ring.at[way, distance - 1, half],
                        down if way else up,
                    ).wait_send()
        for slot in range(8):
            ref = wb.at[z, half, c]
            remote(ref, ref, s_sib.at[slot, half], r_sib.at[z, half], sibling).wait_send()
    for k in range(8):
        if k:
            remote(done.at[k], ob.at[u, t], s_o.at[k, 0], r_o.at[u, t], (dp, ahead(k), t)).wait_send()
        remote(done.at[k], ob.at[u, t], s_o.at[k, 1], r_o.at[u, t], (dp, ahead(k), 1 - t)).wait_send()


def on_device(queries, key_vectors, value_vectors, window_tiles, out_weight):
    dma = pltpu.SemaphoreType.DMA
    bf16, f32 = jnp.bfloat16, jnp.float32
    return pl.pallas_call(
        kernel,
        out_shape=jax.ShapeDtypeStruct((TILE, 1536), bf16),
        in_specs=[pl.BlockSpec(memory_space=pltpu.SMEM)] + [pl.BlockSpec(memory_space=pl.ANY)] * 4,
        out_specs=pl.BlockSpec(memory_space=pltpu.VMEM),
        scratch_shapes=[
            pltpu.VMEM((8, TILE, HD), bf16),
            pltpu.VMEM((8, TILE, HD), bf16),
            pltpu.VMEM((8, TILE, HD), bf16),
            pltpu.VMEM((8, 2, TILE, HD), bf16),
            pltpu.VMEM((8, TILE, HD), bf16),
            pltpu.VMEM((8, 2, 2, 64, 1536), bf16),
            pltpu.VMEM((TILE, WMAX * TILE), f32),
            pltpu.VMEM((TILE, 1536), f32),
            dma((3, 8)), dma((3, 8)), dma((8,)), dma((2, 4)),
            dma((2, 4, 2)), dma((2, 4, 2)), dma((8, 2)), dma((8, 2)), dma((8, 2)), dma((8, 2)),
            pltpu.SemaphoreType.REGULAR, pltpu.SemaphoreType.REGULAR,
        ],
        compiler_params=pltpu.CompilerParams(
            collective_id=0, has_side_effects=True, vmem_limit_bytes=60 << 20
        ),
        name="tile_attention",
    )(window_tiles, queries, key_vectors, value_vectors, out_weight)


def solution(mesh):
    in_specs = (
        P(("dp", "ulysses"), "tensor"),
        P(("dp", "ulysses"), "tensor"),
        P(("dp", "ulysses"), "tensor"),
        P("dp", None),
        P("tensor", "ulysses"),
    )
    out_specs = P(("dp", "ulysses"), "tensor")
    return jax.shard_map(
        on_device, mesh=mesh, in_specs=in_specs, out_specs=out_specs, check_vma=False
    )
```

```python
import functools
import math

import jax
import jax.numpy as jnp
from jax import lax
from jax.experimental import pallas as pl
from jax.experimental.pallas import tpu as pltpu
from jax.sharding import PartitionSpec as P

HD = 128
TILE = 384
WMAX = 6
MESH = pl.DeviceIdType.MESH
COEF = HD ** (-0.5) * math.log2(math.e)
FAR = 1e30


def attend(tile, count, window, q_tile, k_tiles, v_tiles, scores, put):
    first = 2 * jnp.maximum(lax.div(tile, 2) - 1, 0)
    away = []
    for j in range(count):
        listed = window[tile, 0] == first + j
        for s in range(1, WMAX):
            listed = listed | (window[tile, s] == first + j)
        away.append(jnp.where(listed, 0.0, FAR).astype(jnp.float32))
    q = q_tile[tile]
    peak = None
    for j in range(count):
        s = lax.dot_general(
            q, k_tiles[first + j], (((1,), (1,)), ((), ())), preferred_element_type=jnp.float32
        )
        scores[:, pl.ds(j * TILE, TILE)] = s
        top = jnp.maximum(jnp.maximum(s[:, :HD], s[:, HD : 2 * HD]), s[:, 2 * HD :]) - away[j]
        peak = top if peak is None else jnp.maximum(peak, top)
    peak = jnp.max(peak, axis=1, keepdims=True) * COEF
    total = None
    mixed = None
    for j in range(count):
        e = jnp.exp2(scores[:, pl.ds(j * TILE, TILE)] * COEF - (peak + away[j]))
        part = e[:, :HD] + e[:, HD : 2 * HD] + e[:, 2 * HD :]
        total = part if total is None else total + part
        term = jnp.dot(
            e.astype(jnp.bfloat16), v_tiles[first + j], preferred_element_type=jnp.float32
        )
        mixed = term if mixed is None else mixed + term
    total = jnp.sum(total, axis=1, keepdims=True)
    put((mixed / total).astype(jnp.bfloat16))


def kernel(
    window, q_ref, k_ref, v_ref, w_ref, out_ref,
    qb, kb, vb, ob, done, wb, scores, acc,
    s_qkv, r_qkv, s_w, r_w, s_ring, r_ring, s_sib, r_sib, s_o, r_o, level, ready, result, s_out,
):
    dp, u, t = lax.axis_index("dp"), lax.axis_index("ulysses"), lax.axis_index("tensor")
    z, c = lax.div(dp, 2), lax.rem(dp, 2)
    y, w = lax.div(u, 2), lax.rem(u, 2)

    def ahead(k):
        return lax.rem(y + lax.div(k, 2), 4) * 2 + lax.rem(w + lax.rem(k, 2), 2)

    def behind(k):
        return lax.rem(y + 4 - lax.div(k, 2), 4) * 2 + lax.rem(w + lax.rem(k, 2), 2)

    up = (lax.rem(z + 1, 8) * 2 + c, u, t)
    down = (lax.rem(z + 7, 8) * 2 + c, u, t)
    sibling = (z * 2 + 1 - c, u, t)

    barrier = pltpu.get_barrier_semaphore()
    odd = lax.rem(z, 2)

    def tell(sem, device):
        pl.semaphore_signal(sem, inc=1, device_id=device, device_id_type=MESH)

    for k in range(8):
        for other in range(2):
            if k or other:
                tell(barrier, (dp, ahead(k), lax.rem(t + other, 2)))
    tell(barrier, sibling)

    @pl.when(odd == 0)
    def _():
        tell(barrier, up)
        tell(barrier, down)

    pl.semaphore_wait(barrier, 16 + 2 * odd)

    @pl.when(odd == 1)
    def _():
        tell(ready, up)
        tell(ready, down)

    def remote(src, dst, send, recv, device):
        return pltpu.make_async_remote_copy(
            src_ref=src, dst_ref=dst, send_sem=send, recv_sem=recv, device_id=device, device_id_type=MESH
        )

    def landed(ref, sem):
        pltpu.make_async_copy(ref, ref, sem).wait()

    side, place = lax.div(u, 4), lax.rem(u, 4)
    piece = w_ref.at[pl.ds(pl.multiple_of(z * 128 + c * 64, 64), 64), :]
    spot = wb.at[z, t, c, :, pl.ds(pl.multiple_of(place * 384, 384), 384)]
    own = side == t

    @pl.when(own)
    def _():
        pltpu.make_async_copy(piece, spot, r_w.at[t, place]).start()

    @pl.when(jnp.logical_not(own))
    def _():
        remote(piece, spot, s_w.at[0], r_w.at[t, place], (dp, u, side)).start()

    for k in range(1, 8):
        remote(piece, spot, s_w.at[k], r_w.at[t, place], (dp, ahead(k), side)).start()

    for k in range(1, 8):
        remote(piece, spot, s_w.at[k], r_w.at[t, place], (dp, ahead(k), side)).wait_send()

    @pl.when(jnp.logical_not(own))
    def _():
        remote(piece, spot, s_w.at[0], r_w.at[t, place], (dp, u, side)).wait_send()

    x = 2 * w + t
    for step in (1, 3):
        beside = lax.rem(x + step, 4)
        tell(level, (dp, 2 * y + lax.div(beside, 2), lax.rem(beside, 2)))
        tell(level, (dp, 2 * lax.rem(y + step, 4) + w, t))
    pl.semaphore_wait(level, 4)

    arrays = ((k_ref, kb), (v_ref, vb), (q_ref, qb))

    def cut(ref, i):
        return ref.at[:, pl.ds(pl.multiple_of(i * HD, HD), HD)]

    def send(a):
        ref, buf = arrays[a]
        pltpu.make_async_copy(cut(ref, u), buf.at[u], r_qkv.at[a, u]).start()
        for k in range(1, 8):
            remote(
                cut(ref, behind(k)), buf.at[u], s_qkv.at[a, k], r_qkv.at[a, u], (dp, behind(k), t)
            ).start()

    def have(a):
        for i in range(8):
            landed(arrays[a][1].at[i], r_qkv.at[a, i])

    for a in range(3):
        send(a)

    def share(plane, half, slot):
        ref = wb.at[plane, half, c]
        remote(ref, ref, s_sib.at[slot, half], r_sib.at[plane, half], sibling).start()

    def pass_on(plane, half, way, distance):
        ref = wb.at[plane, half, c]
        remote(
            ref, ref, s_ring.at[way, distance - 1, half], r_ring.at[way, distance - 1, half],
            down if way else up,
        ).start()

    for half in range(2):
        for i in range(4):
            landed(wb.at[z, half, c, :, pl.ds(i * 384, 384)], r_w.at[half, i])

    @pl.when(odd == 0)
    def _():
        pl.semaphore_wait(ready, 2)

    for half in range(2):
        pass_on(z, half, 0, 1)
        pass_on(z, half, 1, 1)
    for half in range(2):
        share(z, half, 0)

    def ring(distance):
        for half in range(2):
            for way in range(2):
                if distance == 4 and half != way:
                    continue
                plane = lax.rem(z + (distance if way else 8 - distance), 8)
                landed(wb.at[plane, half, c], r_ring.at[way, distance - 1, half])
                if distance < 3 or (distance == 3 and half == way):
                    pass_on(plane, half, way, distance + 1)
                slot = 4 if distance == 4 else distance + 4 * way
                share(plane, half, slot)

    ring(1)
    acc[...] = jnp.zeros_like(acc)
    have(0)
    have(1)
    ring(2)

    def step(i, carry):
        k = lax.rem(i * 5, 8)
        tile = ahead(k)
        landed(qb.at[tile], r_qkv.at[2, tile])

        def put(value):
            done[k] = value

        edge = (tile < 2) | (tile >= 6)

        @pl.when(edge)
        def _():
            attend(tile, 4, window, qb, kb, vb, scores, put)

        @pl.when(jnp.logical_not(edge))
        def _():
            attend(tile, 6, window, qb, kb, vb, scores, put)

        @pl.when(k == 0)
        def _():
            pltpu.make_async_copy(done.at[k], ob.at[u, t], r_o.at[u, t]).start()

        @pl.when(k > 0)
        def _():
            remote(done.at[k], ob.at[u, t], s_o.at[k, 0], r_o.at[u, t], (dp, tile, t)).start()

        remote(done.at[k], ob.at[u, t], s_o.at[k, 1], r_o.at[u, t], (dp, tile, 1 - t)).start()
        for distance, at in ((3, 3),):

            @pl.when(i == at)
            def _():
                ring(distance)

        return carry

    lax.fori_loop(0, 8, step, 0)

    ring(4)
    for plane in range(8):
        for half in range(2):
            landed(wb.at[plane, half, 1 - c], r_sib.at[plane, half])

    def product(ks, columns):
        sources = [behind(lax.rem(k * 5, 8)) for k in ks]
        rows = jnp.concatenate([ob[source, half] for source in sources for half in range(2)], axis=1)
        part = [wb[source, :, :, :, columns].reshape(256, 512) for source in sources]
        return jnp.dot(rows, jnp.concatenate(part, axis=0), preferred_element_type=jnp.float32)

    def arrived(k):
        source = behind(lax.rem(k * 5, 8))
        for half in range(2):
            landed(ob.at[source, half], r_o.at[source, half])

    def project(g, carry):
        arrived(2 * g)
        arrived(2 * g + 1)
        for n in range(3):
            columns = pl.ds(n * 512, 512)
            acc[:, columns] += product((2 * g, 2 * g + 1), columns)
        return carry

    lax.fori_loop(0, 3, project, 0)
    arrived(6)
    for n in range(3):
        columns = pl.ds(n * 512, 512)
        acc[:, columns] += product((6,), columns)
    arrived(7)
    for n in range(3):
        columns = pl.ds(n * 512, 512)
        result[:, columns] = (acc[:, columns] + product((7,), columns)).astype(jnp.bfloat16)
        pltpu.make_async_copy(result.at[:, columns], out_ref.at[:, columns], s_out.at[n]).start()

    for n in range(3):
        columns = pl.ds(n * 512, 512)
        pltpu.make_async_copy(result.at[:, columns], out_ref.at[:, columns], s_out.at[n]).wait()

    for a, (ref, buf) in enumerate(arrays):
        for k in range(1, 8):
            remote(
                cut(ref, behind(k)), buf.at[u], s_qkv.at[a, k], r_qkv.at[a, u], (dp, behind(k), t)
            ).wait_send()
    for half in range(2):
        for way in range(2):
            for distance in range(1, 5):
                if distance < 4 or half == way:
                    ref = wb.at[z, half, c]
                    remote(
                        ref, ref, s_ring.at[way, distance - 1, half], r_ring.at[way, distance - 1, half],
                        down if way else up,
                    ).wait_send()
        for slot in range(8):
            ref = wb.at[z, half, c]
            remote(ref, ref, s_sib.at[slot, half], r_sib.at[z, half], sibling).wait_send()
    for k in range(8):
        if k:
            remote(done.at[k], ob.at[u, t], s_o.at[k, 0], r_o.at[u, t], (dp, ahead(k), t)).wait_send()
        remote(done.at[k], ob.at[u, t], s_o.at[k, 1], r_o.at[u, t], (dp, ahead(k), 1 - t)).wait_send()


def on_device(queries, key_vectors, value_vectors, window_tiles, out_weight):
    dma = pltpu.SemaphoreType.DMA
    bf16, f32 = jnp.bfloat16, jnp.float32
    return pl.pallas_call(
        kernel,
        out_shape=jax.ShapeDtypeStruct((TILE, 1536), bf16),
        in_specs=[pl.BlockSpec(memory_space=pltpu.SMEM)] + [pl.BlockSpec(memory_space=pl.ANY)] * 4,
        out_specs=pl.BlockSpec(memory_space=pl.ANY),
        scratch_shapes=[
            pltpu.VMEM((8, TILE, HD), bf16),
            pltpu.VMEM((8, TILE, HD), bf16),
            pltpu.VMEM((8, TILE, HD), bf16),
            pltpu.VMEM((8, 2, TILE, HD), bf16),
            pltpu.VMEM((8, TILE, HD), bf16),
            pltpu.VMEM((8, 2, 2, 64, 1536), bf16),
            pltpu.VMEM((TILE, WMAX * TILE), f32),
            pltpu.VMEM((TILE, 1536), f32),
            dma((3, 8)), dma((3, 8)), dma((8,)), dma((2, 4)),
            dma((2, 4, 2)), dma((2, 4, 2)), dma((8, 2)), dma((8, 2)), dma((8, 2)), dma((8, 2)),
            pltpu.SemaphoreType.REGULAR, pltpu.SemaphoreType.REGULAR,
            pltpu.VMEM((TILE, 1536), bf16), dma((3,)),
        ],
        compiler_params=pltpu.CompilerParams(
            collective_id=0, has_side_effects=True, vmem_limit_bytes=60 << 20
        ),
        name="tile_attention",
    )(window_tiles, queries, key_vectors, value_vectors, out_weight)


def solution(mesh):
    in_specs = (
        P(("dp", "ulysses"), "tensor"),
        P(("dp", "ulysses"), "tensor"),
        P(("dp", "ulysses"), "tensor"),
        P("dp", None),
        P("tensor", "ulysses"),
    )
    out_specs = P(("dp", "ulysses"), "tensor")
    return jax.shard_map(
        on_device, mesh=mesh, in_specs=in_specs, out_specs=out_specs, check_vma=False
    )
```

```python
import functools
import math

import jax
import jax.numpy as jnp
from jax import lax
from jax.experimental import pallas as pl
from jax.experimental.pallas import tpu as pltpu
from jax.sharding import PartitionSpec as P

HD = 128
TILE = 384
WMAX = 6
MESH = pl.DeviceIdType.MESH
COEF = HD ** (-0.5) * math.log2(math.e)
FAR = 1e30
ORDER = (0, 5, 2, 7, 4, 1, 6, 3)


def attend(tile, count, window, q_tile, k_tiles, v_tiles, scores, put):
    first = 2 * jnp.maximum(lax.div(tile, 2) - 1, 0)
    away = []
    for j in range(count):
        listed = window[tile, 0] == first + j
        for s in range(1, WMAX):
            listed = listed | (window[tile, s] == first + j)
        away.append(jnp.where(listed, 0.0, FAR).astype(jnp.float32))
    q = q_tile[tile]
    peak = None
    for j in range(count):
        s = lax.dot_general(
            q, k_tiles[first + j], (((1,), (1,)), ((), ())), preferred_element_type=jnp.float32
        )
        scores[:, pl.ds(j * TILE, TILE)] = s
        top = jnp.maximum(jnp.maximum(s[:, :HD], s[:, HD : 2 * HD]), s[:, 2 * HD :]) - away[j]
        peak = top if peak is None else jnp.maximum(peak, top)
    peak = jnp.max(peak, axis=1, keepdims=True) * COEF
    total = None
    mixed = None
    for j in range(count):
        e = jnp.exp2(scores[:, pl.ds(j * TILE, TILE)] * COEF - (peak + away[j]))
        part = e[:, :HD] + e[:, HD : 2 * HD] + e[:, 2 * HD :]
        total = part if total is None else total + part
        term = jnp.dot(
            e.astype(jnp.bfloat16), v_tiles[first + j], preferred_element_type=jnp.float32
        )
        mixed = term if mixed is None else mixed + term
    total = jnp.sum(total, axis=1, keepdims=True)
    put((mixed / total).astype(jnp.bfloat16))


def kernel(
    window, q_ref, k_ref, v_ref, w_ref, out_ref,
    qb, kb, vb, ob, done, wb, scores, acc,
    s_qkv, r_qkv, s_w, r_w, s_ring, r_ring, s_sib, r_sib, s_o, r_o, level, ready, result, s_out,
):
    dp, u, t = lax.axis_index("dp"), lax.axis_index("ulysses"), lax.axis_index("tensor")
    z, c = lax.div(dp, 2), lax.rem(dp, 2)
    y, w = lax.div(u, 2), lax.rem(u, 2)

    def ahead(k):
        return lax.rem(y + lax.div(k, 2), 4) * 2 + lax.rem(w + lax.rem(k, 2), 2)

    def behind(k):
        return lax.rem(y + 4 - lax.div(k, 2), 4) * 2 + lax.rem(w + lax.rem(k, 2), 2)

    up = (lax.rem(z + 1, 8) * 2 + c, u, t)
    down = (lax.rem(z + 7, 8) * 2 + c, u, t)
    sibling = (z * 2 + 1 - c, u, t)

    barrier = pltpu.get_barrier_semaphore()
    odd = lax.rem(z, 2)

    def tell(sem, device):
        pl.semaphore_signal(sem, inc=1, device_id=device, device_id_type=MESH)

    for k in range(8):
        for other in range(2):
            if k or other:
                tell(barrier, (dp, ahead(k), lax.rem(t + other, 2)))
    tell(barrier, sibling)

    @pl.when(odd == 0)
    def _():
        tell(barrier, up)
        tell(barrier, down)

    pl.semaphore_wait(barrier, 16 + 2 * odd)

    @pl.when(odd == 1)
    def _():
        tell(ready, up)
        tell(ready, down)

    def remote(src, dst, send, recv, device):
        return pltpu.make_async_remote_copy(
            src_ref=src, dst_ref=dst, send_sem=send, recv_sem=recv, device_id=device, device_id_type=MESH
        )

    def landed(ref, sem):
        pltpu.make_async_copy(ref, ref, sem).wait()

    side, place = lax.div(u, 4), lax.rem(u, 4)
    piece = w_ref.at[pl.ds(pl.multiple_of(z * 128 + c * 64, 64), 64), :]
    spot = wb.at[z, t, c, :, pl.ds(pl.multiple_of(place * 384, 384), 384)]
    own = side == t

    @pl.when(own)
    def _():
        pltpu.make_async_copy(piece, spot, r_w.at[t, place]).start()

    @pl.when(jnp.logical_not(own))
    def _():
        remote(piece, spot, s_w.at[0], r_w.at[t, place], (dp, u, side)).start()

    for k in range(1, 8):
        remote(piece, spot, s_w.at[k], r_w.at[t, place], (dp, ahead(k), side)).start()

    for k in range(1, 8):
        remote(piece, spot, s_w.at[k], r_w.at[t, place], (dp, ahead(k), side)).wait_send()

    @pl.when(jnp.logical_not(own))
    def _():
        remote(piece, spot, s_w.at[0], r_w.at[t, place], (dp, u, side)).wait_send()

    x = 2 * w + t
    for step in (1, 3):
        beside = lax.rem(x + step, 4)
        tell(level, (dp, 2 * y + lax.div(beside, 2), lax.rem(beside, 2)))
        tell(level, (dp, 2 * lax.rem(y + step, 4) + w, t))
    pl.semaphore_wait(level, 4)

    arrays = ((k_ref, kb), (v_ref, vb), (q_ref, qb))

    def cut(ref, i):
        return ref.at[:, pl.ds(pl.multiple_of(i * HD, HD), HD)]

    def send(a):
        ref, buf = arrays[a]
        for k in range(1, 8):
            remote(
                cut(ref, behind(k)), buf.at[u], s_qkv.at[a, k], r_qkv.at[a, u], (dp, behind(k), t)
            ).start()

    def have(a):
        for i in range(8):
            landed(arrays[a][1].at[i], r_qkv.at[a, i])

    for a in range(3):
        send(a)
    for ref, buf, sem in ((k_ref, kb, 0), (v_ref, vb, 1), (q_ref, qb, 2)):
        pltpu.make_async_copy(cut(ref, u), buf.at[u], r_qkv.at[sem, u]).start()

    def share(plane, half, slot):
        ref = wb.at[plane, half, c]
        remote(ref, ref, s_sib.at[slot, half], r_sib.at[plane, half], sibling).start()

    def pass_on(plane, half, way, distance):
        ref = wb.at[plane, half, c]
        remote(
            ref, ref, s_ring.at[way, distance - 1, half], r_ring.at[way, distance - 1, half],
            down if way else up,
        ).start()

    for half in range(2):
        for i in range(4):
            landed(wb.at[z, half, c, :, pl.ds(i * 384, 384)], r_w.at[half, i])

    @pl.when(odd == 0)
    def _():
        pl.semaphore_wait(ready, 2)

    for half in range(2):
        pass_on(z, half, 0, 1)
        pass_on(z, half, 1, 1)
    for half in range(2):
        share(z, half, 0)

    def ring(distance):
        for half in range(2):
            for way in range(2):
                if distance == 4 and half != way:
                    continue
                plane = lax.rem(z + (distance if way else 8 - distance), 8)
                landed(wb.at[plane, half, c], r_ring.at[way, distance - 1, half])
                if distance < 3 or (distance == 3 and half == way):
                    pass_on(plane, half, way, distance + 1)
                slot = 4 if distance == 4 else distance + 4 * way
                share(plane, half, slot)

    ring(1)
    acc[...] = jnp.zeros_like(acc)
    have(0)
    have(1)
    ring(2)

    def step(i, orders):
        k = lax.rem(orders, 8)
        tile = ahead(k)
        landed(qb.at[tile], r_qkv.at[2, tile])

        def put(value):
            done[k] = value

        edge = (tile < 2) | (tile >= 6)

        @pl.when(edge)
        def _():
            attend(tile, 4, window, qb, kb, vb, scores, put)

        @pl.when(jnp.logical_not(edge))
        def _():
            attend(tile, 6, window, qb, kb, vb, scores, put)

        @pl.when(k == 0)
        def _():
            pltpu.make_async_copy(done.at[k], ob.at[u, t], r_o.at[u, t]).start()

        @pl.when(k > 0)
        def _():
            remote(done.at[k], ob.at[u, t], s_o.at[k, 0], r_o.at[u, t], (dp, tile, t)).start()

        remote(done.at[k], ob.at[u, t], s_o.at[k, 1], r_o.at[u, t], (dp, tile, 1 - t)).start()
        for distance, at in ((3, 3),):

            @pl.when(i == at)
            def _():
                ring(distance)

        return lax.div(orders, 8)

    lax.fori_loop(0, 8, step, sum(k * 8**i for i, k in enumerate(ORDER)))

    ring(4)
    for plane in range(8):
        for half in range(2):
            landed(wb.at[plane, half, 1 - c], r_sib.at[plane, half])

    def product(sources, columns):
        rows = jnp.concatenate([ob[source, half] for source in sources for half in range(2)], axis=1)
        part = [wb[source, :, :, :, columns].reshape(256, 512) for source in sources]
        return jnp.dot(rows, jnp.concatenate(part, axis=0), preferred_element_type=jnp.float32)

    def arrived(source):
        for half in range(2):
            landed(ob.at[source, half], r_o.at[source, half])

    def project(g, orders):
        sources = behind(lax.rem(orders, 8)), behind(lax.rem(lax.div(orders, 8), 8))
        for source in sources:
            arrived(source)
        for n in range(3):
            columns = pl.ds(n * 512, 512)
            acc[:, columns] += product(sources, columns)
        return lax.div(orders, 64)

    lax.fori_loop(0, 3, project, sum(k * 8**i for i, k in enumerate(ORDER)))
    for place in (6, 7):
        source = behind(ORDER[place])
        arrived(source)
        for n in range(3):
            columns = pl.ds(n * 512, 512)
            total = acc[:, columns] + product((source,), columns)
            if place == 6:
                acc[:, columns] = total
            else:
                result[:, columns] = total.astype(jnp.bfloat16)
                pltpu.make_async_copy(result.at[:, columns], out_ref.at[:, columns], s_out.at[n]).start()

    for n in range(3):
        columns = pl.ds(n * 512, 512)
        pltpu.make_async_copy(result.at[:, columns], out_ref.at[:, columns], s_out.at[n]).wait()

    for a, (ref, buf) in enumerate(arrays):
        for k in range(1, 8):
            remote(
                cut(ref, behind(k)), buf.at[u], s_qkv.at[a, k], r_qkv.at[a, u], (dp, behind(k), t)
            ).wait_send()
    for half in range(2):
        for way in range(2):
            for distance in range(1, 5):
                if distance < 4 or half == way:
                    ref = wb.at[z, half, c]
                    remote(
                        ref, ref, s_ring.at[way, distance - 1, half], r_ring.at[way, distance - 1, half],
                        down if way else up,
                    ).wait_send()
        for slot in range(8):
            ref = wb.at[z, half, c]
            remote(ref, ref, s_sib.at[slot, half], r_sib.at[z, half], sibling).wait_send()
    for k in range(8):
        if k:
            remote(done.at[k], ob.at[u, t], s_o.at[k, 0], r_o.at[u, t], (dp, ahead(k), t)).wait_send()
        remote(done.at[k], ob.at[u, t], s_o.at[k, 1], r_o.at[u, t], (dp, ahead(k), 1 - t)).wait_send()


def hand_over(source, target, held, s_in, s_out):
    parts = [pl.ds(i * 96, 96) for i in range(4)]
    reads = [pltpu.make_async_copy(source.at[p], held.at[p], s_in.at[i]) for i, p in enumerate(parts)]
    writes = [pltpu.make_async_copy(held.at[p], target.at[p], s_out.at[i]) for i, p in enumerate(parts)]
    for read in reads:
        read.start()
    for read, write in zip(reads, writes):
        read.wait()
        write.start()
    for write in writes:
        write.wait()


def on_device(queries, key_vectors, value_vectors, window_tiles, out_weight):
    dma = pltpu.SemaphoreType.DMA
    bf16, f32 = jnp.bfloat16, jnp.float32
    mixed = pl.pallas_call(
        kernel,
        out_shape=jax.ShapeDtypeStruct((TILE, 1536), bf16),
        in_specs=[pl.BlockSpec(memory_space=pltpu.SMEM)] + [pl.BlockSpec(memory_space=pl.ANY)] * 4,
        out_specs=pl.BlockSpec(memory_space=pl.ANY),
        scratch_shapes=[
            pltpu.VMEM((8, TILE, HD), bf16),
            pltpu.VMEM((8, TILE, HD), bf16),
            pltpu.VMEM((8, TILE, HD), bf16),
            pltpu.VMEM((8, 2, TILE, HD), bf16),
            pltpu.VMEM((8, TILE, HD), bf16),
            pltpu.VMEM((8, 2, 2, 64, 1536), bf16),
            pltpu.VMEM((TILE, WMAX * TILE), f32),
            pltpu.VMEM((TILE, 1536), f32),
            dma((3, 8)), dma((3, 8)), dma((8,)), dma((2, 4)),
            dma((2, 4, 2)), dma((2, 4, 2)), dma((8, 2)), dma((8, 2)), dma((8, 2)), dma((8, 2)),
            pltpu.SemaphoreType.REGULAR, pltpu.SemaphoreType.REGULAR,
            pltpu.VMEM((TILE, 1536), bf16), dma((3,)),
        ],
        compiler_params=pltpu.CompilerParams(
            collective_id=0, has_side_effects=True, vmem_limit_bytes=60 << 20
        ),
        name="tile_attention",
    )(window_tiles, queries, key_vectors, value_vectors, out_weight)
    return pl.pallas_call(
        hand_over,
        out_shape=jax.ShapeDtypeStruct((TILE, 1536), bf16),
        in_specs=[pl.BlockSpec(memory_space=pl.ANY)],
        out_specs=pl.BlockSpec(memory_space=pl.ANY),
        scratch_shapes=[pltpu.VMEM((TILE, 1536), bf16), dma((4,)), dma((4,))],
        name="hand_over",
    )(mixed)


def solution(mesh):
    in_specs = (
        P(("dp", "ulysses"), "tensor"),
        P(("dp", "ulysses"), "tensor"),
        P(("dp", "ulysses"), "tensor"),
        P("dp", None),
        P("tensor", "ulysses"),
    )
    out_specs = P(("dp", "ulysses"), "tensor")
    return jax.shard_map(
        on_device, mesh=mesh, in_specs=in_specs, out_specs=out_specs, check_vma=False
    )
```

```python
import functools
import math

import jax
import jax.numpy as jnp
from jax import lax
from jax.experimental import pallas as pl
from jax.experimental.pallas import tpu as pltpu
from jax.sharding import PartitionSpec as P

HD = 128
TILE = 384
WMAX = 6
MESH = pl.DeviceIdType.MESH
COEF = HD ** (-0.5) * math.log2(math.e)
FAR = 1e30
ORDER = (0, 5, 2, 7, 4, 1, 6, 3)


def attend(tile, count, window, q_tile, k_tiles, v_tiles, scores, put):
    first = 2 * jnp.maximum(lax.div(tile, 2) - 1, 0)
    away = []
    for j in range(count):
        listed = window[tile, 0] == first + j
        for s in range(1, WMAX):
            listed = listed | (window[tile, s] == first + j)
        away.append(jnp.where(listed, 0.0, FAR).astype(jnp.float32))
    q = q_tile[tile]
    peak = None
    for j in range(count):
        s = lax.dot_general(
            q, k_tiles[first + j], (((1,), (1,)), ((), ())), preferred_element_type=jnp.float32
        )
        scores[:, pl.ds(j * TILE, TILE)] = s
        top = jnp.maximum(jnp.maximum(s[:, :HD], s[:, HD : 2 * HD]), s[:, 2 * HD :]) - away[j]
        peak = top if peak is None else jnp.maximum(peak, top)
    peak = jnp.max(peak, axis=1, keepdims=True) * COEF
    total = None
    mixed = None
    for j in range(count):
        e = jnp.exp2(scores[:, pl.ds(j * TILE, TILE)] * COEF - (peak + away[j]))
        part = e[:, :HD] + e[:, HD : 2 * HD] + e[:, 2 * HD :]
        total = part if total is None else total + part
        term = jnp.dot(
            e.astype(jnp.bfloat16), v_tiles[first + j], preferred_element_type=jnp.float32
        )
        mixed = term if mixed is None else mixed + term
    total = jnp.sum(total, axis=1, keepdims=True)
    put((mixed / total).astype(jnp.bfloat16))


def kernel(
    window, q_ref, k_ref, v_ref, w_ref, out_ref,
    qb, kb, vb, ob, done, wb, scores, acc,
    s_qkv, r_qkv, s_w, r_w, s_ring, r_ring, s_sib, r_sib, s_o, r_o, level, ready, result, s_out,
):
    dp, u, t = lax.axis_index("dp"), lax.axis_index("ulysses"), lax.axis_index("tensor")
    z, c = lax.div(dp, 2), lax.rem(dp, 2)
    y, w = lax.div(u, 2), lax.rem(u, 2)

    def ahead(k):
        return lax.rem(y + lax.div(k, 2), 4) * 2 + lax.rem(w + lax.rem(k, 2), 2)

    def behind(k):
        return lax.rem(y + 4 - lax.div(k, 2), 4) * 2 + lax.rem(w + lax.rem(k, 2), 2)

    up = (lax.rem(z + 1, 8) * 2 + c, u, t)
    down = (lax.rem(z + 7, 8) * 2 + c, u, t)
    sibling = (z * 2 + 1 - c, u, t)

    barrier = pltpu.get_barrier_semaphore()
    odd = lax.rem(z, 2)

    def tell(sem, device):
        pl.semaphore_signal(sem, inc=1, device_id=device, device_id_type=MESH)

    for k in range(8):
        for other in range(2):
            if k or other:
                tell(barrier, (dp, ahead(k), lax.rem(t + other, 2)))
    tell(barrier, sibling)

    @pl.when(odd == 0)
    def _():
        tell(barrier, up)
        tell(barrier, down)

    pl.semaphore_wait(barrier, 16 + 2 * odd)

    @pl.when(odd == 1)
    def _():
        tell(ready, up)
        tell(ready, down)

    def remote(src, dst, send, recv, device):
        return pltpu.make_async_remote_copy(
            src_ref=src, dst_ref=dst, send_sem=send, recv_sem=recv, device_id=device, device_id_type=MESH
        )

    def landed(ref, sem):
        pltpu.make_async_copy(ref, ref, sem).wait()

    side, place = lax.div(u, 4), lax.rem(u, 4)
    piece = w_ref.at[pl.ds(pl.multiple_of(z * 128 + c * 64, 64), 64), :]
    spot = wb.at[z, t, c, :, pl.ds(pl.multiple_of(place * 384, 384), 384)]
    own = side == t

    @pl.when(own)
    def _():
        pltpu.make_async_copy(piece, spot, r_w.at[t, place]).start()

    @pl.when(jnp.logical_not(own))
    def _():
        remote(piece, spot, s_w.at[0], r_w.at[t, place], (dp, u, side)).start()

    for k in range(1, 8):
        remote(piece, spot, s_w.at[k], r_w.at[t, place], (dp, ahead(k), side)).start()

    for k in range(1, 8):
        remote(piece, spot, s_w.at[k], r_w.at[t, place], (dp, ahead(k), side)).wait_send()

    @pl.when(jnp.logical_not(own))
    def _():
        remote(piece, spot, s_w.at[0], r_w.at[t, place], (dp, u, side)).wait_send()

    x = 2 * w + t
    for step in (1, 3):
        beside = lax.rem(x + step, 4)
        tell(level, (dp, 2 * y + lax.div(beside, 2), lax.rem(beside, 2)))
        tell(level, (dp, 2 * lax.rem(y + step, 4) + w, t))
    pl.semaphore_wait(level, 4)

    arrays = ((k_ref, kb), (v_ref, vb), (q_ref, qb))

    def cut(ref, i):
        return ref.at[:, pl.ds(pl.multiple_of(i * HD, HD), HD)]

    def send(a):
        ref, buf = arrays[a]
        for k in range(1, 8):
            remote(
                cut(ref, behind(k)), buf.at[u], s_qkv.at[a, k], r_qkv.at[a, u], (dp, behind(k), t)
            ).start()

    def have(a):
        for i in range(8):
            landed(arrays[a][1].at[i], r_qkv.at[a, i])

    for a in range(3):
        send(a)
    for ref, buf, sem in ((k_ref, kb, 0), (v_ref, vb, 1), (q_ref, qb, 2)):
        pltpu.make_async_copy(cut(ref, u), buf.at[u], r_qkv.at[sem, u]).start()

    def share(plane, half, slot):
        ref = wb.at[plane, half, c]
        remote(ref, ref, s_sib.at[slot, half], r_sib.at[plane, half], sibling).start()

    def pass_on(plane, half, way, distance):
        ref = wb.at[plane, half, c]
        remote(
            ref, ref, s_ring.at[way, distance - 1, half], r_ring.at[way, distance - 1, half],
            down if way else up,
        ).start()

    for half in range(2):
        for i in range(4):
            landed(wb.at[z, half, c, :, pl.ds(i * 384, 384)], r_w.at[half, i])

    @pl.when(odd == 0)
    def _():
        pl.semaphore_wait(ready, 2)

    for half in range(2):
        pass_on(z, half, 0, 1)
        pass_on(z, half, 1, 1)
    for half in range(2):
        share(z, half, 0)

    def ring(distance):
        for half in range(2):
            for way in range(2):
                if distance == 4 and half != way:
                    continue
                plane = lax.rem(z + (distance if way else 8 - distance), 8)
                landed(wb.at[plane, half, c], r_ring.at[way, distance - 1, half])
                if distance < 3 or (distance == 3 and half == way):
                    pass_on(plane, half, way, distance + 1)
                slot = 4 if distance == 4 else distance + 4 * way
                share(plane, half, slot)

    ring(1)
    acc[...] = jnp.zeros_like(acc)
    have(0)
    have(1)
    ring(2)

    def step(i, orders):
        k = lax.rem(orders, 8)
        tile = ahead(k)
        landed(qb.at[tile], r_qkv.at[2, tile])

        def put(value):
            done[k] = value

        edge = (tile < 2) | (tile >= 6)

        @pl.when(edge)
        def _():
            attend(tile, 4, window, qb, kb, vb, scores, put)

        @pl.when(jnp.logical_not(edge))
        def _():
            attend(tile, 6, window, qb, kb, vb, scores, put)

        @pl.when(k == 0)
        def _():
            pltpu.make_async_copy(done.at[k], ob.at[u, t], r_o.at[u, t]).start()

        @pl.when(k > 0)
        def _():
            remote(done.at[k], ob.at[u, t], s_o.at[k, 0], r_o.at[u, t], (dp, tile, t)).start()

        remote(done.at[k], ob.at[u, t], s_o.at[k, 1], r_o.at[u, t], (dp, tile, 1 - t)).start()
        for distance, at in ((3, 3),):

            @pl.when(i == at)
            def _():
                ring(distance)

        return lax.div(orders, 8)

    lax.fori_loop(0, 8, step, sum(k * 8**i for i, k in enumerate(ORDER)))

    ring(4)
    def product(sources, columns):
        rows = jnp.concatenate([ob[source, half] for source in sources for half in range(2)], axis=1)
        part = [wb[source, :, :, :, columns].reshape(256, 512) for source in sources]
        return jnp.dot(rows, jnp.concatenate(part, axis=0), preferred_element_type=jnp.float32)

    def arrived(source):
        for half in range(2):
            landed(wb.at[source, half, 1 - c], r_sib.at[source, half])
            landed(ob.at[source, half], r_o.at[source, half])

    def project(g, orders):
        sources = behind(lax.rem(orders, 8)), behind(lax.rem(lax.div(orders, 8), 8))
        for source in sources:
            arrived(source)
        for n in range(3):
            columns = pl.ds(n * 512, 512)
            acc[:, columns] += product(sources, columns)
        return lax.div(orders, 64)

    lax.fori_loop(0, 3, project, sum(k * 8**i for i, k in enumerate(ORDER)))
    for place in (6, 7):
        source = behind(ORDER[place])
        arrived(source)
        for n in range(3):
            columns = pl.ds(n * 512, 512)
            total = acc[:, columns] + product((source,), columns)
            if place == 6:
                acc[:, columns] = total
            else:
                result[:, columns] = total.astype(jnp.bfloat16)
                pltpu.make_async_copy(result.at[:, columns], out_ref.at[:, columns], s_out.at[n]).start()

    for n in range(3):
        columns = pl.ds(n * 512, 512)
        pltpu.make_async_copy(result.at[:, columns], out_ref.at[:, columns], s_out.at[n]).wait()

    for a, (ref, buf) in enumerate(arrays):
        for k in range(1, 8):
            remote(
                cut(ref, behind(k)), buf.at[u], s_qkv.at[a, k], r_qkv.at[a, u], (dp, behind(k), t)
            ).wait_send()
    for half in range(2):
        for way in range(2):
            for distance in range(1, 5):
                if distance < 4 or half == way:
                    ref = wb.at[z, half, c]
                    remote(
                        ref, ref, s_ring.at[way, distance - 1, half], r_ring.at[way, distance - 1, half],
                        down if way else up,
                    ).wait_send()
        for slot in range(8):
            ref = wb.at[z, half, c]
            remote(ref, ref, s_sib.at[slot, half], r_sib.at[z, half], sibling).wait_send()
    for k in range(8):
        if k:
            remote(done.at[k], ob.at[u, t], s_o.at[k, 0], r_o.at[u, t], (dp, ahead(k), t)).wait_send()
        remote(done.at[k], ob.at[u, t], s_o.at[k, 1], r_o.at[u, t], (dp, ahead(k), 1 - t)).wait_send()


def hand_over(source, target, held, s_in, s_out):
    parts = [pl.ds(i * 96, 96) for i in range(4)]
    reads = [pltpu.make_async_copy(source.at[p], held.at[p], s_in.at[i]) for i, p in enumerate(parts)]
    writes = [pltpu.make_async_copy(held.at[p], target.at[p], s_out.at[i]) for i, p in enumerate(parts)]
    for read in reads:
        read.start()
    for read, write in zip(reads, writes):
        read.wait()
        write.start()
    for write in writes:
        write.wait()


def on_device(queries, key_vectors, value_vectors, window_tiles, out_weight):
    dma = pltpu.SemaphoreType.DMA
    bf16, f32 = jnp.bfloat16, jnp.float32
    mixed = pl.pallas_call(
        kernel,
        out_shape=jax.ShapeDtypeStruct((TILE, 1536), bf16),
        in_specs=[pl.BlockSpec(memory_space=pltpu.SMEM)] + [pl.BlockSpec(memory_space=pl.ANY)] * 4,
        out_specs=pl.BlockSpec(memory_space=pl.ANY),
        scratch_shapes=[
            pltpu.VMEM((8, TILE, HD), bf16),
            pltpu.VMEM((8, TILE, HD), bf16),
            pltpu.VMEM((8, TILE, HD), bf16),
            pltpu.VMEM((8, 2, TILE, HD), bf16),
            pltpu.VMEM((8, TILE, HD), bf16),
            pltpu.VMEM((8, 2, 2, 64, 1536), bf16),
            pltpu.VMEM((TILE, WMAX * TILE), f32),
            pltpu.VMEM((TILE, 1536), f32),
            dma((3, 8)), dma((3, 8)), dma((8,)), dma((2, 4)),
            dma((2, 4, 2)), dma((2, 4, 2)), dma((8, 2)), dma((8, 2)), dma((8, 2)), dma((8, 2)),
            pltpu.SemaphoreType.REGULAR, pltpu.SemaphoreType.REGULAR,
            pltpu.VMEM((TILE, 1536), bf16), dma((3,)),
        ],
        compiler_params=pltpu.CompilerParams(
            collective_id=0, has_side_effects=True, vmem_limit_bytes=60 << 20
        ),
        name="tile_attention",
    )(window_tiles, queries, key_vectors, value_vectors, out_weight)
    return pl.pallas_call(
        hand_over,
        out_shape=jax.ShapeDtypeStruct((TILE, 1536), bf16),
        in_specs=[pl.BlockSpec(memory_space=pl.ANY)],
        out_specs=pl.BlockSpec(memory_space=pl.ANY),
        scratch_shapes=[pltpu.VMEM((TILE, 1536), bf16), dma((4,)), dma((4,))],
        name="hand_over",
    )(mixed)


def solution(mesh):
    in_specs = (
        P(("dp", "ulysses"), "tensor"),
        P(("dp", "ulysses"), "tensor"),
        P(("dp", "ulysses"), "tensor"),
        P("dp", None),
        P("tensor", "ulysses"),
    )
    out_specs = P(("dp", "ulysses"), "tensor")
    return jax.shard_map(
        on_device, mesh=mesh, in_specs=in_specs, out_specs=out_specs, check_vma=False
    )
```
